256 devices in a mesh: teacher: 8 (over x, z_hi), tensor: 16 (over y, z_lo), student: 2 (over core).
Axes of the slice: x: 4, y: 4, z: 8 (z_hi: 2, z_lo: 4; z = z_hi * 4 + z_lo), core: 2. Of those that a mesh axis runs over, the one named last changes fastest.
Arguments:
- teacher_hidden: bfloat16 [4096, 16384], P(('teacher', 'student'), 'tensor'), may hold values from -1800 to 1800
- norm_gain: bfloat16 [16384], P('tensor'), may hold values from 0.5 to 1.5
- projector: bfloat16 [16384, 4096], P('tensor'), may hold values from -0.0625 to 0.0625
- doc_lengths: int32 [16, 16], replicated, may hold values from 1 to 40, 256 in all within a row
- doc_student: int32 [16, 16], replicated, may hold values from 0 to 15, each once within a row
- student_resid: bfloat16 [10240, 4096], P(('teacher', 'student'), 'tensor'), may hold values from -6 to 6
- student_attn: bfloat16 [10240, 4096], P(('teacher', 'student'), 'tensor'), may hold values from -6 to 6
- out_weight: bfloat16 [4096, 4096], P(None, 'tensor'), may hold values from -0.125 to 0.125
Outputs:
- act_grad: bfloat16 [10240, 4096], P(('teacher', 'student'), 'tensor')
- weight_grad: bfloat16 [4096, 4096], P(None, 'tensor')
The draws below stay inside these ranges and needn't reach their ends.
Inputs may be any that keep to these rules, and one draw needn't show every extreme that they name: `doc_lengths`: row g lists the lengths of the 16 documents of teacher sequence g in order; each row sums to 256. doc_student[g, c] is the student replica that trains on document c of sequence g; each row names every replica once.
All inputs are finite; a program needn't handle non-finite values.
Results may differ from the reference program's by a relative error of at most 0.005.
Values may be sent and summed in bfloat16 or wider, within the bound.
No kernel may reach another device: no remote copies, remote signals or barrier semaphores. Data moves between devices by JAX's collectives and lax.ppermute only.
A program may use at most 128 MiB of HBM per device.

```python
import math
import jax
import jax.numpy as jnp
import numpy as np
from jax import lax

DT = 16384
DS = 4096
TOK = 256
NGROUPS = 16
SLOT = 40
ROWS = 4096
SROWS = 10240


def draw_teacher_hidden(key, part):
    key = jax.random.fold_in(key, 11)
    row_key, column_key, base_key = jax.random.split(key, 3)
    row_scale = 10.0 ** jax.random.uniform(row_key, (ROWS, 1), jnp.float32)
    ramp = jnp.arange(DT, dtype=jnp.float32) / DT
    column_scale = 10.0 ** jax.random.uniform(column_key, (1, DT), jnp.float32) * (3.0 ** ramp)[None, :]
    base = jnp.clip(jax.random.normal(base_key, (ROWS, DT), jnp.float32), -6.0, 6.0)
    return (base * row_scale * column_scale).astype(jnp.bfloat16)


def with_spikes(drawn, rng, source, target, blocks, factor):
    def block_of(axis_at):
        return (jnp.arange(drawn.shape[axis_at]) // (drawn.shape[axis_at] // blocks)).reshape((-1,) + (1,) * (drawn.ndim - 1 - axis_at))

    near = jax.random.permutation(rng, blocks)[block_of(target)]
    second = (block_of(target) + blocks // 2) % blocks
    return jnp.where((block_of(source) == near) | (block_of(source) == second), factor * drawn, drawn)


def steps_of(stream_key, shape, cuts, low, high):
    gain = 1.0
    for dim, blocks in cuts:
        draws = jax.random.uniform(jax.random.fold_in(jax.random.fold_in(stream_key, 6), dim), (blocks,), jnp.float32, low / len(cuts), high / len(cuts))
        gain = gain * jnp.repeat(jnp.exp(draws), shape[dim] // blocks).reshape((-1,) + (1,) * (len(shape) - 1 - dim))
    return gain


def length_profile(number_of, total, limit, skew):
    loads = [(1 << 20) // math.isqrt(rank ** skew) + 1 for rank in range(2, number_of + 1)]
    rest, holding = total - limit - (number_of - 1), [1] * (number_of - 1)
    while rest > 0:
        movable = [i for i in range(number_of - 1) if holding[i] < limit]
        whole, remaining = sum([loads[i] for i in movable]), rest
        for i in movable:
            addition = min(limit - holding[i], max(1, remaining * loads[i] // whole), rest)
            holding[i] = holding[i] + addition
            rest = rest - addition
    return np.array([limit] + holding)


def ragged_sizes(stream_key, number_of, total, most, skew):
    if number_of == 2:
        one = jax.random.randint(stream_key, (), max(1, total - most), min(most, total - 1) + 1)
        return jnp.stack([one, total - one])
    lengths = jnp.asarray(length_profile(number_of, total, most, skew), jnp.int32)
    twos = (number_of - 1) // 2
    donor, sink = lengths[1:1 + 2 * twos:2], lengths[2:2 + 2 * twos:2]
    room = jnp.minimum(donor - 1, most - sink)
    moved = jax.random.randint(jax.random.fold_in(stream_key, 1), (twos,), 0, 1 << 20) % (room + 1)
    lengths = lengths.at[1:1 + 2 * twos:2].set(donor - moved).at[2:2 + 2 * twos:2].set(sink + moved)
    return lengths[jax.random.permutation(jax.random.fold_in(stream_key, 2), number_of)]


def centred(own_key, shape, deviation, limit, cuts=(), kind=jnp.bfloat16):
    gain = steps_of(own_key, shape, cuts, -0.22, 0.18) if cuts else 1.0
    result = jax.random.normal(own_key, shape, jnp.float32) * deviation * gain
    return jnp.minimum(jnp.maximum(result, -limit), limit).astype(kind)


def gaussian_with(rng, shape, spread, most, cuts, heavy, kind=jnp.bfloat16):
    values = spread * jax.random.normal(rng, shape, jnp.float32)
    if cuts:
        values = values * steps_of(rng, shape, cuts, -0.22, 0.18)
    return jnp.clip(with_spikes(values, jax.random.fold_in(rng, 3), *heavy), -most, most).astype(kind)


def setup_inputs(seed: int = 0) -> dict:
    streams_of = jax.random.split(jax.random.key(seed), 9)
    teacher_hidden = draw_teacher_hidden(jax.random.fold_in(streams_of[8], 71), 0)
    norm_gain = jnp.clip(1.0 + 0.1 * jax.random.normal(streams_of[1], (DT,), jnp.float32), 0.5, 1.5).astype(jnp.bfloat16)
    projector = gaussian_with(streams_of[2], (DT, DS), DT ** -0.5, 0.0625, ((0, 16),), (0, 1, 16, 2.0))
    doc_lengths = jax.vmap(lambda own: ragged_sizes(own, NGROUPS, TOK, SLOT, 2))(jax.random.split(streams_of[3], NGROUPS)).reshape((NGROUPS, NGROUPS)).astype(jnp.int32)
    doc_student = jax.vmap(lambda own: jax.random.permutation(own, NGROUPS))(jax.random.split(streams_of[4], NGROUPS)).reshape((NGROUPS, NGROUPS)).astype(jnp.int32)
    student_resid = centred(streams_of[5], (SROWS, DS), 1.0, 6.0, ((0, 16), (1, 16)))
    student_attn = centred(streams_of[6], (SROWS, DS), 1.0, 6.0, ((0, 16), (1, 16)))
    out_weight = gaussian_with(streams_of[7], (DS, DS), DS ** -0.5, 0.125, ((1, 16),), (1, 0, 16, 2.0))
    return {"teacher_hidden": teacher_hidden, "norm_gain": norm_gain, "projector": projector, "doc_lengths": doc_lengths, "doc_student": doc_student, "student_resid": student_resid, "student_attn": student_attn, "out_weight": out_weight}


def project_group(group_rows, norm_gain, projector):
    wide = group_rows.astype(jnp.float32)
    power = lax.optimization_barrier(jnp.sum(wide * wide, axis=1, keepdims=True))
    normed = (wide * lax.rsqrt(power / DT + 1e-05) * norm_gain.astype(jnp.float32)).astype(jnp.bfloat16)
    return jnp.dot(normed, projector, preferred_element_type=jnp.float32)

def reference(teacher_hidden, norm_gain, projector, doc_lengths, doc_student, student_resid, student_attn, out_weight):
    target = lax.map(lambda group_rows: project_group(group_rows, norm_gain, projector), teacher_hidden.reshape(NGROUPS, TOK, DT))
    offsets = (jnp.cumsum(doc_lengths, axis=1) - doc_lengths).astype(jnp.int32)
    replicas = jnp.arange(NGROUPS, dtype=jnp.int32)
    onehot = (doc_student[:, :, None] == replicas[None, None, :]).astype(jnp.int32)
    length_to = lax.optimization_barrier(jnp.sum(onehot * doc_lengths[:, :, None], axis=1)).astype(jnp.int32)
    offset_to = lax.optimization_barrier(jnp.sum(onehot * offsets[:, :, None], axis=1)).astype(jnp.int32)
    position = jnp.arange(SLOT, dtype=jnp.int32)
    live = position[None, None, :] < length_to[:, :, None]
    gather_index = jnp.where(live, offset_to[:, :, None] + position[None, None, :], 0).astype(jnp.int32)
    picked = jax.vmap(lambda table, where_from: table[where_from.reshape(-1)])(target, gather_index)
    picked = picked.reshape(NGROUPS, NGROUPS, SLOT, DS)
    picked = jnp.where(live[..., None], picked, jnp.zeros((), jnp.float32))
    arranged = jnp.transpose(picked, (1, 0, 2, 3)).reshape(SROWS, DS)
    live_rows = jnp.transpose(live, (1, 0, 2)).reshape(SROWS, 1)
    student_out = student_resid.astype(jnp.float32) + jnp.dot(student_attn, out_weight, preferred_element_type=jnp.float32)
    residual = jnp.where(live_rows, student_out - arranged.astype(jnp.float32), 0.0).astype(jnp.bfloat16)
    act_grad = jnp.dot(residual, out_weight.T, preferred_element_type=jnp.float32).astype(jnp.bfloat16)
    weight_sum = jnp.dot(student_attn.T, residual, preferred_element_type=jnp.float32)
    weight_grad = (weight_sum / (NGROUPS * TOK)).astype(jnp.bfloat16)
    return (act_grad, weight_grad)
```

```python
import jax
import jax.numpy as jnp
from jax import lax
from jax.experimental import pallas as pl
from jax.experimental.pallas import tpu as pltpu
from jax.sharding import Mesh
from jax.sharding import PartitionSpec as P

DT = 16384
EPS = 1e-05
GROUP = ("x", "zh", "core")
TENSOR = ("y", "zl")
BF = jnp.bfloat16
F32 = jnp.float32
VMEM_LIMIT = 40 * 1024 * 1024


def ring(n, k):
    return [(i, (i + k) % n) for i in range(n)]


SWAP = [(0, 1), (1, 0)]


def eye_mask(n):
    return lax.broadcasted_iota(jnp.int32, (n, n), 0) == lax.broadcasted_iota(jnp.int32, (n, n), 1)


def split_rows(row):
    high = row.astype(BF).astype(F32)
    rest = row - high
    middle = rest.astype(BF).astype(F32)
    low = rest - middle
    at = lax.broadcasted_iota(jnp.int32, (16, row.shape[1]), 0)
    return jnp.where(at == 0, high, jnp.where(at == 1, middle, jnp.where(at == 2, low, 0.0))).astype(BF)


def project_kernel(place, hidden, gain, projector, *rest):
    outs, scaled = rest[:4], rest[4]
    step = pl.program_id(0)
    rows = hidden.shape[0]

    @pl.when(step == 0)
    def _():
        wide = hidden[...].astype(F32)
        scaled[...] = (wide * gain[...].astype(F32)).astype(BF)
        power = jnp.sum(wide * wide, axis=1, keepdims=True)
        parts = split_rows(jnp.sum(jnp.where(eye_mask(rows), power, 0.0), axis=0, keepdims=True))
        for out in outs:
            out[rows:, :rows] = parts
            out[rows:, rows:] = jnp.zeros((16, out.shape[1] - rows), BF)

    for i, out in enumerate(outs):

        @pl.when(step == i)
        def _(out=out):
            out[:rows, :] = jnp.dot(scaled[...], projector[...], preferred_element_type=F32).astype(BF)


def project(y, hidden, gain, projector):
    rows, depth = hidden.shape
    width = projector.shape[1] // 4
    return pl.pallas_call(
        project_kernel,
        grid_spec=pltpu.PrefetchScalarGridSpec(
            num_scalar_prefetch=1,
            grid=(4,),
            in_specs=[
                pl.BlockSpec((rows, depth), lambda i, s: (0, 0)),
                pl.BlockSpec((1, depth), lambda i, s: (0, 0)),
                pl.BlockSpec((depth, width), lambda i, s: (0, (s[0] + i) % 4)),
            ],
            out_specs=[pl.BlockSpec((rows + 16, width), lambda i, s: (0, 0))] * 4,
            scratch_shapes=[pltpu.VMEM((rows, depth), BF)],
        ),
        out_shape=[jax.ShapeDtypeStruct((rows + 16, width), BF)] * 4,
        compiler_params=pltpu.CompilerParams(vmem_limit_bytes=VMEM_LIMIT),
        cost_estimate=pl.CostEstimate(
            flops=2 * rows * depth * 4 * width, bytes_accessed=2 * depth * 4 * width, transcendentals=0
        ),
        name="project",
    )(y.reshape(1), hidden, gain.reshape(1, depth), projector)


def fold_kernel(place, a, b, c, d, *outs):
    rows = a.shape[0] - 16
    width = outs[0].shape[1]
    total = sum(r[rows:, :rows].astype(F32) for r in (a, b, c, d))
    parts = split_rows(jnp.sum(total, axis=0, keepdims=True))
    for k, out in enumerate(outs):
        at = pl.ds(pl.multiple_of(((place[0] + k) % 4) * width, width), width)
        out[:rows, :] = sum(r[:rows, at].astype(F32) for r in (a, b, c, d)).astype(BF)
        out[rows:, :] = parts


def fold(zl, parts):
    rows, width = parts[0].shape[0], parts[0].shape[1] // 4
    vmem = pl.BlockSpec(memory_space=pltpu.VMEM)
    return pl.pallas_call(
        fold_kernel,
        in_specs=[pl.BlockSpec(memory_space=pltpu.SMEM)] + [vmem] * 4,
        out_specs=[vmem] * 4,
        out_shape=[jax.ShapeDtypeStruct((rows, width), BF)] * 4,
        compiler_params=pltpu.CompilerParams(vmem_limit_bytes=VMEM_LIMIT),
        name="fold",
    )(zl.reshape(1), *parts)


def middle_kernel(place, attn, weight, resid, a, b, c, d, g0, g1, g2, g3, keep, send):
    rows = resid.shape[0]
    y, core = place[0], place[1]
    total = sum(r[:rows, :].astype(F32) for r in (a, b, c, d))
    power = jnp.sum(sum(r[rows:, :].astype(F32) for r in (a, b, c, d)), axis=0, keepdims=True)
    power = jnp.sum(jnp.where(eye_mask(rows), power, 0.0), axis=1, keepdims=True)
    value = resid[...].astype(F32) - total * lax.rsqrt(power / DT + EPS)
    for t in range(16):
        value += jnp.dot(attn[t], weight[t], preferred_element_type=F32)
    residual = value.astype(BF)
    for k, out in enumerate((g0, g1, g2, g3)):
        for z in range(4):
            w = weight[((y + k) % 4) * 4 + z]
            out[z] = lax.dot_general(
                residual, w, (((1,), (1,)), ((), ())), preferred_element_type=F32
            ).astype(BF)
    for out, half in ((keep, core), (send, 1 - core)):
        for i in range(8):
            out[i] = lax.dot_general(
                attn[half * 8 + i], residual, (((0,), (0,)), ((), ())), preferred_element_type=F32
            ).astype(out.dtype)


def middle(place, attn, weight, resid, parts):
    rows = resid.shape[0]
    vmem = pl.BlockSpec(memory_space=pltpu.VMEM)
    return pl.pallas_call(
        middle_kernel,
        in_specs=[pl.BlockSpec(memory_space=pltpu.SMEM)] + [vmem] * 7,
        out_specs=[vmem] * 6,
        out_shape=[jax.ShapeDtypeStruct((4, rows, 256), BF)] * 4
        + [jax.ShapeDtypeStruct((8, 256, 256), F32)] * 2,
        compiler_params=pltpu.CompilerParams(vmem_limit_bytes=VMEM_LIMIT),
        name="middle",
    )(place, attn, weight, resid, *parts)


def exchange(pieces, axis):
    return [pieces[0]] + [lax.ppermute(pieces[k], axis, ring(4, k)) for k in (1, 2, 3)]


def add_up(pieces):
    return sum(p.astype(F32) for p in pieces)


def body(hidden, gain, projector, doc_lengths, doc_student, resid, attn, weight):
    groups, slot = 16, resid.shape[0] // 16
    rows = hidden.shape[0]
    me = lax.axis_index(GROUP)
    x, y, zl, core = (lax.axis_index(a) for a in ("x", "y", "zl", "core"))

    offsets = jnp.cumsum(doc_lengths, axis=1) - doc_lengths
    matches = (doc_student[me][:, None] == jnp.arange(groups, dtype=jnp.int32)[None, :]).astype(jnp.int32)
    length = jnp.sum(matches * doc_lengths[me][:, None], axis=0)
    offset = jnp.sum(matches * offsets[me][:, None], axis=0)
    position = jnp.arange(slot, dtype=jnp.int32)
    where = jnp.where(position[None, :] < length[:, None], offset[:, None] + position[None, :], -1).reshape(-1)
    select = (jnp.arange(rows, dtype=jnp.int32)[:, None] == where[None, :]).astype(BF)

    def to_sequence(slots):
        got = lax.all_to_all(slots.reshape(groups, slot, -1), GROUP, 0, 0, tiled=True)
        return jnp.dot(select, got.reshape(groups * slot, -1), preferred_element_type=F32).astype(BF)

    attn_rows = to_sequence(attn)
    resid_rows = to_sequence(resid)

    parts = exchange(project(y, hidden, gain, projector), "y")
    parts = exchange(fold(zl, parts), "zl")

    gathered = lax.all_gather(attn_rows, "zl", axis=0, tiled=True)
    gathered = lax.all_gather(gathered, "y", axis=0, tiled=True)

    g0, g1, g2, g3, keep, send = middle(
        jnp.stack([y, core]),
        gathered.reshape(16, rows, 256),
        weight.reshape(16, 256, 256),
        resid_rows,
        parts,
    )

    grads = exchange([g0, g1, g2, g3], "y")
    grads = [
        add_up([lax.dynamic_index_in_dim(g, (zl + k) % 4, 0, keepdims=False) for g in grads]).astype(BF)
        for k in range(4)
    ]
    grad = add_up(exchange(grads, "zl")).astype(BF)
    slots = lax.dot_general(select, grad, (((0,), (0,)), ((), ())), preferred_element_type=F32).astype(BF)
    act_grad = lax.all_to_all(slots.reshape(groups, slot, -1), GROUP, 0, 0, tiled=True).reshape(resid.shape)

    other = lax.ppermute(send, "core", SWAP)
    pieces = [
        (
            lax.dynamic_slice_in_dim(keep, ((x + k) % 4) * 2, 2, 0)
            + lax.dynamic_slice_in_dim(other, ((x + k) % 4) * 2, 2, 0)
        ).astype(BF)
        for k in range(4)
    ]
    own = lax.reduce_precision(add_up(exchange(pieces, "x")), 8, 7)
    far = lax.ppermute(own.astype(BF), "zh", SWAP)
    done = ((own + far.astype(F32)) / (groups * rows)).astype(BF)
    half = lax.all_gather(done.reshape(512, 256), "x", axis=0, tiled=True)
    twin = lax.ppermute(half, "core", SWAP)
    first = jnp.where(core == 0, half, twin)
    second = jnp.where(core == 0, twin, half)
    weight_grad = jnp.concatenate([first, second], axis=0)
    return act_grad, weight_grad


def solution(mesh):
    fine = Mesh(mesh.devices.reshape(4, 2, 4, 4, 2), ("x", "zh", "y", "zl", "core"))
    return jax.shard_map(
        body,
        mesh=fine,
        in_specs=(
            P(GROUP, TENSOR),
            P(TENSOR),
            P(TENSOR, None),
            P(),
            P(),
            P(GROUP, TENSOR),
            P(GROUP, TENSOR),
            P(None, TENSOR),
        ),
        out_specs=(P(GROUP, TENSOR), P(None, TENSOR)),
        check_vma=False,
    )
```

```python
import functools

import jax
import jax.numpy as jnp
from jax import lax
from jax.experimental import pallas as pl
from jax.experimental.pallas import tpu as pltpu
from jax.sharding import Mesh
from jax.sharding import PartitionSpec as P

DT = 16384
EPS = 1e-05
GROUP = ("x", "zh", "core")
TENSOR = ("y", "zl")
BF = jnp.bfloat16
F32 = jnp.float32
B = 256
VMEM = pl.BlockSpec(memory_space=pltpu.VMEM)
SMEM = pl.BlockSpec(memory_space=pltpu.SMEM)
PARAMS = pltpu.CompilerParams(vmem_limit_bytes=24 * 1024 * 1024)
SWAP = [(0, 1), (1, 0)]


def ring(k):
    return [(i, (i + k) % 4) for i in range(4)]


def tie(*groups):
    return lax.optimization_barrier(groups)


def shape(*dims, dtype=BF):
    return jax.ShapeDtypeStruct(dims, dtype)


def eye_mask(n):
    return lax.broadcasted_iota(jnp.int32, (n, n), 0) == lax.broadcasted_iota(jnp.int32, (n, n), 1)


def power_rows(row, dtype):
    at = lax.broadcasted_iota(jnp.int32, (16, row.shape[1]), 0)
    if dtype == F32:
        return jnp.where(at == 0, row, 0.0)
    high = row.astype(BF).astype(F32)
    rest = row - high
    middle = rest.astype(BF).astype(F32)
    low = rest - middle
    return jnp.where(at == 0, high, jnp.where(at == 1, middle, jnp.where(at == 2, low, 0.0))).astype(BF)


def piece_of(outs, k, j):
    up, down, near_up, near_down, rest_up, rest_down, own = outs
    if k == 0:
        return own, j
    if k == 1:
        return (near_up, j) if j < 2 else (rest_up, j - 2)
    if k == 2:
        return (up, j) if j < 2 else (down, j - 2)
    return (rest_down, j) if j < 2 else (near_down, j - 2)


def piece_shapes(rows):
    return [shape(2, rows, B)] * 2 + [shape(2, rows, B, dtype=F32)] * 2 + [shape(2, rows, B)] * 2 + [shape(4, rows, B, dtype=F32)]


def project_kernel(place, hidden, gain, projector, *rest):
    outs, scaled, blocks, sems = rest[:7], rest[7], rest[8], rest[9]
    y, zl = place[0], place[1]
    width = blocks.shape[2]
    copies = []
    for k in range(4):
        at = pl.ds(pl.multiple_of(((y + k) % 4) * width, width), width)
        copies.append(pltpu.make_async_copy(projector.at[:, at], blocks.at[k], sems.at[k]))
        copies[k].start()
    wide = hidden[...].astype(F32)
    scaled[...] = (wide * gain[...].astype(F32)).astype(BF)
    power = jnp.sum(wide * wide, axis=1, keepdims=True)
    power = jnp.sum(jnp.where(eye_mask(B), power, 0.0), axis=0, keepdims=True)
    for out in outs:
        rows = power_rows(power, out.dtype)
        for i in range(out.shape[0]):
            out[i, B:, :] = rows
    for k in range(4):
        copies[k].wait()
        for j in range(4):
            out, i = piece_of(outs, k, j)
            at = pl.ds(pl.multiple_of(((zl + j) % 4) * B, B), B)
            out[i, :B, :] = jnp.dot(scaled[...], blocks[k, :, at], preferred_element_type=F32).astype(out.dtype)


def project(place, hidden, gain, projector):
    rows, depth = hidden.shape
    width = projector.shape[1] // 4
    return pl.pallas_call(
        project_kernel,
        in_specs=[SMEM, VMEM, VMEM, pl.BlockSpec(memory_space=pltpu.HBM)],
        out_specs=[VMEM] * 7,
        out_shape=piece_shapes(rows + 16),
        scratch_shapes=[
            pltpu.VMEM((rows, depth), BF),
            pltpu.VMEM((4, depth, width), BF),
            pltpu.SemaphoreType.DMA((4,)),
        ],
        compiler_params=pltpu.CompilerParams(vmem_limit_bytes=48 * 1024 * 1024),
        cost_estimate=pl.CostEstimate(
            flops=2 * rows * depth * 4 * width, bytes_accessed=2 * depth * 4 * width, transcendentals=0
        ),
        name="project",
    )(place, hidden, gain.reshape(1, depth), projector)


def put_sum(out, at, terms):
    rows = terms[0].shape[0]
    total = sum(t[:B, :].astype(F32) for t in terms).astype(out.dtype)
    if at is None:
        out[:B, :] = total
    else:
        out[at, :B, :] = total
    if rows > B:
        power = sum(jnp.sum(t[B:, :].astype(F32), axis=0, keepdims=True) for t in terms)
        power = power_rows(power, out.dtype)
        if at is None:
            out[B:, :] = power
        else:
            out[at, B:, :] = power


def relay_kernel(near_up, near_down, rest_up, rest_down, got_up, got_down, up, down):
    for i in range(2):
        put_sum(up, i, [near_up.at[i], got_up.at[i]])
        put_sum(down, 2 + i, [near_down.at[i], got_down.at[i]])
        up[2 + i] = rest_up[i]
        down[i] = rest_down[i]


def relay(*parts):
    rows = parts[0].shape[1]
    return pl.pallas_call(
        relay_kernel,
        in_specs=[VMEM] * 6,
        out_specs=[VMEM] * 2,
        out_shape=[shape(4, rows, B)] * 2,
        compiler_params=PARAMS,
        name="relay",
    )(*parts)


def fold_kernel(own, far_up, far_down, *outs):
    for j, out in enumerate(outs):
        put_sum(out, None, [own.at[j], far_up.at[j], far_down.at[j]])


def fold(*parts):
    rows = parts[0].shape[1]
    return pl.pallas_call(
        fold_kernel,
        in_specs=[VMEM] * 3,
        out_specs=[VMEM] * 4,
        out_shape=[shape(rows, B, dtype=F32)] + [shape(rows, B)] * 3,
        compiler_params=PARAMS,
        name="fold",
    )(*parts)


def middle_kernel(place, a0, a1, a2, a3, weight, resid, t0, t1, t2, t3, *outs):
    pieces, keep, send = outs[:7], outs[7], outs[8]
    y, zl, core = place[0], place[1], place[2]
    attn = (a0, a1, a2, a3)
    parts = (t0, t1, t2, t3)
    total = sum(r[:B, :].astype(F32) for r in parts)
    power = jnp.sum(sum(r[B:, :].astype(F32) for r in parts), axis=0, keepdims=True)
    power = jnp.sum(jnp.where(eye_mask(B), power, 0.0), axis=1, keepdims=True)
    value = resid[...].astype(F32) - total * lax.rsqrt(power / DT + EPS)
    for k in range(4):
        for j in range(4):
            w = weight[((y + 4 - k) % 4) * 4 + (zl + 4 - j) % 4]
            value += jnp.dot(attn[k][j], w, preferred_element_type=F32)
    residual = value.astype(BF)
    for k in range(4):
        for j in range(4):
            out, i = piece_of(pieces, k, j)
            w = weight[((y + k) % 4) * 4 + (zl + j) % 4]
            out[i] = lax.dot_general(
                residual, w, (((1,), (1,)), ((), ())), preferred_element_type=F32
            ).astype(out.dtype)
    for half in range(2):

        @pl.when(core == half)
        def _(half=half):
            for m in range(16):
                out = keep if m // 8 == half else send
                out[m % 8] = lax.dot_general(
                    attn[m // 4][m % 4], residual, (((0,), (0,)), ((), ())), preferred_element_type=F32
                ).astype(out.dtype)


def middle(place, chunks, weight, resid, parts):
    return pl.pallas_call(
        middle_kernel,
        in_specs=[SMEM] + [VMEM] * 10,
        out_specs=[VMEM] * 9,
        out_shape=piece_shapes(B) + [shape(8, B, B, dtype=F32)] * 2,
        compiler_params=PARAMS,
        name="middle",
    )(place, *chunks, weight, resid, *parts)


def pair_kernel(a, b, out):
    out[:, :B] = a[...]
    out[:, B:] = b[...]


def pair(a, b):
    return pl.pallas_call(
        pair_kernel,
        in_specs=[VMEM] * 2,
        out_specs=VMEM,
        out_shape=shape(a.shape[0], 2 * B),
        compiler_params=PARAMS,
        name="pair",
    )(a, b)


def pick_kernel(at, slots, first, second):
    rows = lax.broadcasted_iota(jnp.int32, (B, slots.shape[0]), 0)
    select = jnp.where(rows == at[...], 1.0, 0.0).astype(BF)
    first[...] = jnp.dot(select, slots[:, :B], preferred_element_type=F32).astype(BF)
    second[...] = jnp.dot(select, slots[:, B:], preferred_element_type=F32).astype(BF)


def pick(at, slots):
    return pl.pallas_call(
        pick_kernel,
        in_specs=[VMEM] * 2,
        out_specs=[VMEM] * 2,
        out_shape=[shape(B, B)] * 2,
        compiler_params=PARAMS,
        name="pick",
    )(at.reshape(1, -1), slots.reshape(-1, 2 * B))


def put_kernel(at, a, b, c, d, out):
    grad = sum(r[...].astype(F32) for r in (a, b, c, d)).astype(BF)
    rows = lax.broadcasted_iota(jnp.int32, (out.shape[0], B), 1)
    select = jnp.where(rows == at[...], 1.0, 0.0).astype(BF)
    out[...] = jnp.dot(select, grad, preferred_element_type=F32).astype(BF)


def put(at, parts):
    at = at.reshape(-1)
    return pl.pallas_call(
        put_kernel,
        in_specs=[VMEM] * 5,
        out_specs=VMEM,
        out_shape=shape(at.shape[0], B),
        compiler_params=PARAMS,
        name="put",
    )(at.reshape(-1, 1), *parts)


def join_kernel(*refs):
    out, i = refs[-1], 0
    for ref in refs[:-1]:
        for j in range(ref.shape[0]):
            out[i] = ref[j]
            i += 1


def join(*parts):
    return pl.pallas_call(
        join_kernel,
        in_specs=[VMEM] * len(parts),
        out_specs=VMEM,
        out_shape=shape(sum(p.shape[0] for p in parts), *parts[0].shape[1:]),
        compiler_params=PARAMS,
        name="join",
    )(*parts)


def share_kernel(place, keep, other, *outs):
    for k, out in enumerate(outs):
        for i in range(2):
            at = ((place[3] + k) % 4) * 2 + i
            out[i] = (keep[at] + other[at]).astype(out.dtype)


def share(place, keep, other):
    return pl.pallas_call(
        share_kernel,
        in_specs=[SMEM] + [VMEM] * 2,
        out_specs=[VMEM] * 4,
        out_shape=[shape(2, B, B, dtype=F32)] + [shape(2, B, B)] * 3,
        compiler_params=PARAMS,
        name="share",
    )(place, keep, other)


def total_kernel(scale, *refs):
    refs[-1][...] = (sum(r[...].astype(F32) for r in refs[:-1]) * scale).astype(refs[-1].dtype)


def total(parts, scale=1.0):
    return pl.pallas_call(
        functools.partial(total_kernel, scale),
        in_specs=[VMEM] * len(parts),
        out_specs=VMEM,
        out_shape=shape(*parts[0].shape),
        compiler_params=PARAMS,
        name="total",
    )(*parts)


def assemble_kernel(place, mine, twin, out):
    y, zl, core, x = place[0], place[1], place[2], place[3]
    for s in range(8):
        within = ((x + 4 - s // 2) % 4) * 2 + s % 2
        for source, half in ((mine, core), (twin, 1 - core)):
            m = half * 8 + within
            out[((y + 4 - m // 4) % 4) * 4 + (zl + 4 - m % 4) % 4] = source[s]


def assemble(place, mine, twin):
    return pl.pallas_call(
        assemble_kernel,
        in_specs=[SMEM, VMEM, VMEM],
        out_specs=VMEM,
        out_shape=shape(16, B, B),
        compiler_params=PARAMS,
        name="assemble",
    )(place, mine, twin)


def send_on(piece, axis, k):
    return lax.ppermute(piece, axis, ring(k))


def relay_first(parts):
    return send_on(parts[0], "y", 1), send_on(parts[1], "y", 3)


def relay_second(parts, got):
    up, down = relay(*parts[2:6], *got)
    return send_on(up, "y", 1), send_on(down, "y", 3)


def body(hidden, gain, projector, doc_lengths, doc_student, resid, attn, weight):
    groups, slot = 16, attn.shape[0] // 16
    rows = hidden.shape[0]
    me = lax.axis_index(GROUP)
    x, y, zl, core = (lax.axis_index(a) for a in ("x", "y", "zl", "core"))
    place = jnp.stack([y, zl, core, x])

    offsets = jnp.cumsum(doc_lengths, axis=1) - doc_lengths
    matches = (doc_student[me][:, None] == jnp.arange(groups, dtype=jnp.int32)[None, :]).astype(jnp.int32)
    length = jnp.sum(matches * doc_lengths[me][:, None], axis=0)
    offset = jnp.sum(matches * offsets[me][:, None], axis=0)
    position = jnp.arange(slot, dtype=jnp.int32)
    where = jnp.where(position[None, :] < length[:, None], offset[:, None] + position[None, :], -1)

    both = pair(attn, resid).reshape(groups, slot, 2 * B)
    slots = lax.all_to_all(both, GROUP, 0, 0, tiled=True)
    teacher = project(place, hidden, gain, projector)
    got = relay_first(teacher)
    attn_rows, resid_rows = pick(where, slots)
    got, attn_rows = tie(got, attn_rows)
    along_zl = [attn_rows] + [send_on(attn_rows, "zl", j) for j in (1, 2, 3)]
    far = relay_second(teacher, got)

    chunk = join(*(p[None] for p in along_zl))
    far, chunk = tie(far, chunk)
    chunks = [chunk] + [send_on(chunk, "y", k) for k in (1, 2, 3)]
    folded = fold(teacher[6], *far)
    parts = [folded[0]] + [send_on(folded[j], "zl", j) for j in (1, 2, 3)]

    outs = middle(place, chunks, weight.reshape(16, B, B), resid_rows, parts)
    grads, keep, send = outs[:7], outs[7], outs[8]

    got = relay_first(grads)
    other = lax.ppermute(send, "core", SWAP)
    pieces = share(place, keep, other)
    got, pieces = tie(got, pieces)
    pieces = [pieces[0]] + [send_on(pieces[k], "x", k) for k in (1, 2, 3)]
    far = relay_second(grads, got)

    near = total(pieces)
    away = lax.ppermute(near, "zh", SWAP)
    far, near = tie(far, near)
    folded = fold(grads[6], *far)
    grad_parts = [folded[0]] + [send_on(folded[j], "zl", j) for j in (1, 2, 3)]
    done = total([near, away], 1.0 / (groups * rows))
    after, before = send_on(done, "x", 1), send_on(done, "x", 3)
    grad_parts, after, before = tie(grad_parts, after, before)
    slots = put(where, grad_parts)
    slots = lax.all_to_all(slots.reshape(groups, slot, B), GROUP, 0, 0, tiled=True)
    mine = [done, after, send_on(done, "x", 2), before]
    slots, mine = tie(slots, mine)
    mine = join(*mine)
    twin = lax.ppermute(mine, "core", SWAP)
    weight_grad = assemble(place, mine, twin).reshape(weight.shape)
    return slots.reshape(attn.shape), weight_grad

def solution(mesh):
    fine = Mesh(mesh.devices.reshape(4, 2, 4, 4, 2), ("x", "zh", "y", "zl", "core"))
    return jax.shard_map(
        body,
        mesh=fine,
        in_specs=(
            P(GROUP, TENSOR),
            P(TENSOR),
            P(TENSOR, None),
            P(),
            P(),
            P(GROUP, TENSOR),
            P(GROUP, TENSOR),
            P(None, TENSOR),
        ),
        out_specs=(P(GROUP, TENSOR), P(None, TENSOR)),
        check_vma=False,
    )
```

```python
import functools

import jax
import jax.numpy as jnp
from jax import lax
from jax.experimental import pallas as pl
from jax.experimental.pallas import tpu as pltpu
from jax.sharding import Mesh
from jax.sharding import PartitionSpec as P

DT = 16384
EPS = 1e-05
GROUP = ("x", "zh", "core")
TENSOR = ("y", "zl")
BF = jnp.bfloat16
F32 = jnp.float32
B = 256
VMEM = pl.BlockSpec(memory_space=pltpu.VMEM)
SMEM = pl.BlockSpec(memory_space=pltpu.SMEM)
PARAMS = pltpu.CompilerParams(vmem_limit_bytes=24 * 1024 * 1024)
SWAP = [(0, 1), (1, 0)]


def ring(k):
    return [(i, (i + k) % 4) for i in range(4)]


def tie(*groups):
    return lax.optimization_barrier(groups)


def shape(*dims, dtype=BF):
    return jax.ShapeDtypeStruct(dims, dtype)


def eye_mask(n):
    return lax.broadcasted_iota(jnp.int32, (n, n), 0) == lax.broadcasted_iota(jnp.int32, (n, n), 1)


def power_rows(row, dtype):
    at = lax.broadcasted_iota(jnp.int32, (16, row.shape[1]), 0)
    if dtype == F32:
        return jnp.where(at == 0, row, 0.0)
    high = row.astype(BF).astype(F32)
    rest = row - high
    middle = rest.astype(BF).astype(F32)
    low = rest - middle
    return jnp.where(at == 0, high, jnp.where(at == 1, middle, jnp.where(at == 2, low, 0.0))).astype(BF)


def piece_of(outs, k, j):
    up, down, near_up, near_down, rest_up, rest_down, own = outs
    if k == 0:
        return own, j
    if k == 1:
        return (near_up, j) if j < 2 else (rest_up, j - 2)
    if k == 2:
        return (up, j) if j < 2 else (down, j - 2)
    return (rest_down, j) if j < 2 else (near_down, j - 2)


def heavy_piece_of(outs, k, j):
    up, down, near_up, near_down, own = outs
    if k == 0:
        return own, j
    if k == 1:
        return (near_up, j) if j < 2 else (up, j)
    if k == 2:
        return (up, j) if j < 2 else (down, j - 2)
    return (down, 2 + j) if j < 2 else (near_down, j - 2)


def heavy_shapes(rows):
    return [shape(4, rows, B)] * 2 + [shape(2, rows, B, dtype=F32)] * 2 + [shape(4, rows, B, dtype=F32)]


def piece_shapes(rows):
    return [shape(2, rows, B)] * 2 + [shape(2, rows, B, dtype=F32)] * 2 + [shape(2, rows, B)] * 2 + [shape(4, rows, B, dtype=F32)]


def project_kernel(place, hidden, gain, projector, *rest):
    outs, scaled, held, blocks, sems = rest[:7], rest[7], rest[8], rest[9], rest[10]
    y, zl = place[0], place[1]
    width = blocks.shape[2]
    first = pltpu.make_async_copy(hidden, held, sems.at[4])
    first.start()
    copies = []
    for k in range(4):
        at = pl.ds(pl.multiple_of(((y + k) % 4) * width, width), width)
        copies.append(pltpu.make_async_copy(projector.at[:, at], blocks.at[k], sems.at[k]))
        copies[k].start()
    scale = gain[...].astype(F32)
    scale = jnp.concatenate([scale[i : i + 1, :] for i in range(scale.shape[0])], axis=1)
    first.wait()
    wide = held[...].astype(F32)
    scaled[...] = (wide * scale).astype(BF)
    power = jnp.sum(wide * wide, axis=1, keepdims=True)
    power = jnp.sum(jnp.where(eye_mask(B), power, 0.0), axis=0, keepdims=True)
    for out in outs:
        rows = power_rows(power, out.dtype)
        for i in range(out.shape[0]):
            out[i, B:, :] = rows
    for k in range(4):
        copies[k].wait()
        for j in range(4):
            out, i = piece_of(outs, k, j)
            at = pl.ds(pl.multiple_of(((zl + j) % 4) * B, B), B)
            out[i, :B, :] = jnp.dot(scaled[...], blocks[k, :, at], preferred_element_type=F32).astype(out.dtype)


def project(place, hidden, gain, projector):
    rows, depth = hidden.shape
    width = projector.shape[1] // 4
    hbm = pl.BlockSpec(memory_space=pltpu.HBM)
    return pl.pallas_call(
        project_kernel,
        in_specs=[SMEM, hbm, VMEM, hbm],
        out_specs=[VMEM] * 7,
        out_shape=piece_shapes(rows + 16),
        scratch_shapes=[
            pltpu.VMEM((rows, depth), BF),
            pltpu.VMEM((rows, depth), BF),
            pltpu.VMEM((4, depth, width), BF),
            pltpu.SemaphoreType.DMA((5,)),
        ],
        compiler_params=pltpu.CompilerParams(vmem_limit_bytes=48 * 1024 * 1024),
        cost_estimate=pl.CostEstimate(
            flops=2 * rows * depth * 4 * width, bytes_accessed=2 * depth * 4 * width, transcendentals=0
        ),
        name="project",
    )(place, hidden, gain.reshape(depth // 128, 128), projector)


def put_sum(out, at, terms):
    rows = terms[0].shape[0]
    total = sum(t[:B, :].astype(F32) for t in terms).astype(out.dtype)
    if at is None:
        out[:B, :] = total
    else:
        out[at, :B, :] = total
    if rows > B:
        power = sum(jnp.sum(t[B:, :].astype(F32), axis=0, keepdims=True) for t in terms)
        power = power_rows(power, out.dtype)
        if at is None:
            out[B:, :] = power
        else:
            out[at, B:, :] = power


def relay_kernel(near_up, near_down, rest_up, rest_down, got_up, got_down, up, down):
    for i in range(2):
        put_sum(up, i, [near_up.at[i], got_up.at[i]])
        put_sum(down, 2 + i, [near_down.at[i], got_down.at[i]])
        up[2 + i] = rest_up[i]
        down[i] = rest_down[i]


def relay(*parts):
    rows = parts[0].shape[1]
    return pl.pallas_call(
        relay_kernel,
        in_specs=[VMEM] * 6,
        out_specs=[VMEM] * 2,
        out_shape=[shape(4, rows, B)] * 2,
        compiler_params=PARAMS,
        name="relay",
    )(*parts)


def heavy_relay_kernel(near_up, near_down, got_up, got_down, up, down):
    for i in range(2):
        put_sum(up, i, [near_up.at[i], got_up.at[i]])
        put_sum(down, i, [near_down.at[i], got_down.at[i]])


def heavy_relay(*parts):
    return pl.pallas_call(
        heavy_relay_kernel,
        in_specs=[VMEM] * 4,
        out_specs=[VMEM] * 2,
        out_shape=[shape(2, B, B)] * 2,
        compiler_params=PARAMS,
        name="heavy_relay",
    )(*parts)


def heavy_fold_kernel(own, got_up, got_down, far_up, far_down, *outs):
    for j, out in enumerate(outs):
        got, far = (got_down.at[2 + j], far_up.at[j]) if j < 2 else (got_up.at[j], far_down.at[j - 2])
        put_sum(out, None, [own.at[j], got, far])


def heavy_fold(*parts):
    return pl.pallas_call(
        heavy_fold_kernel,
        in_specs=[VMEM] * 5,
        out_specs=[VMEM] * 4,
        out_shape=[shape(B, B, dtype=F32)] + [shape(B, B)] * 3,
        compiler_params=PARAMS,
        name="heavy_fold",
    )(*parts)


def fold_kernel(own, far_up, far_down, *outs):
    for j, out in enumerate(outs):
        put_sum(out, None, [own.at[j], far_up.at[j], far_down.at[j]])


def fold(*parts):
    rows = parts[0].shape[1]
    return pl.pallas_call(
        fold_kernel,
        in_specs=[VMEM] * 3,
        out_specs=[VMEM] * 4,
        out_shape=[shape(rows, B, dtype=F32)] + [shape(rows, B)] * 3,
        compiler_params=PARAMS,
        name="fold",
    )(*parts)


def middle_kernel(place, a0, a1, a2, a3, weight, at, resid, t0, t1, t2, t3, *outs):
    pieces, keep, send = outs[:5], outs[5], outs[6]
    y, zl, core = place[0], place[1], place[2]
    attn = (a0, a1, a2, a3)
    parts = (t0, t1, t2, t3)
    total = sum(r[:B, :].astype(F32) for r in parts)
    power = jnp.sum(sum(r[B:, :].astype(F32) for r in parts), axis=0, keepdims=True)
    power = jnp.sum(jnp.where(eye_mask(B), power, 0.0), axis=1, keepdims=True)
    rows = lax.broadcasted_iota(jnp.int32, (B, resid.shape[0]), 0)
    select = jnp.where(rows == at[...], 1.0, 0.0).astype(BF)
    value = jnp.dot(select, resid[...], preferred_element_type=F32) - total * lax.rsqrt(power / DT + EPS)
    for k in range(4):
        for j in range(4):
            w = weight[((y + 4 - k) % 4) * 4 + (zl + 4 - j) % 4]
            value += jnp.dot(attn[k][j], w, preferred_element_type=F32)
    residual = value.astype(BF)
    for k in range(4):
        for j in range(4):
            out, i = heavy_piece_of(pieces, k, j)
            w = weight[((y + k) % 4) * 4 + (zl + j) % 4]
            out[i] = lax.dot_general(
                residual, w, (((1,), (1,)), ((), ())), preferred_element_type=F32
            ).astype(out.dtype)
    for half in range(2):

        @pl.when(core == half)
        def _(half=half):
            for m in range(16):
                out = keep if m // 8 == half else send
                out[m % 8] = lax.dot_general(
                    attn[m // 4][m % 4], residual, (((0,), (0,)), ((), ())), preferred_element_type=F32
                ).astype(out.dtype)


def middle(place, chunks, weight, at, resid, parts):
    return pl.pallas_call(
        middle_kernel,
        in_specs=[SMEM] + [VMEM] * 11,
        out_specs=[VMEM] * 7,
        out_shape=heavy_shapes(B) + [shape(8, B, B, dtype=F32)] * 2,
        compiler_params=PARAMS,
        name="middle",
    )(place, *chunks, weight, at.reshape(1, -1), resid.reshape(-1, B), *parts)


def pick_kernel(at, slots, out):
    rows = lax.broadcasted_iota(jnp.int32, (B, slots.shape[0]), 0)
    select = jnp.where(rows == at[...], 1.0, 0.0).astype(BF)
    out[...] = jnp.dot(select, slots[...], preferred_element_type=F32).astype(BF)


def pick(at, slots):
    return pl.pallas_call(
        pick_kernel,
        in_specs=[VMEM] * 2,
        out_specs=VMEM,
        out_shape=shape(B, B),
        compiler_params=PARAMS,
        name="pick",
    )(at.reshape(1, -1), slots.reshape(-1, B))


def put_kernel(at, a, b, c, d, out):
    grad = sum(r[...].astype(F32) for r in (a, b, c, d)).astype(BF)
    rows = lax.broadcasted_iota(jnp.int32, (out.shape[0], B), 1)
    select = jnp.where(rows == at[...], 1.0, 0.0).astype(BF)
    out[...] = jnp.dot(select, grad, preferred_element_type=F32).astype(BF)


def put(at, parts):
    at = at.reshape(-1)
    return pl.pallas_call(
        put_kernel,
        in_specs=[VMEM] * 5,
        out_specs=VMEM,
        out_shape=shape(at.shape[0], B),
        compiler_params=PARAMS,
        name="put",
    )(at.reshape(-1, 1), *parts)


def join_kernel(*refs):
    out, i = refs[-1], 0
    for ref in refs[:-1]:
        for j in range(ref.shape[0]):
            out[i] = ref[j]
            i += 1


def join(*parts):
    return pl.pallas_call(
        join_kernel,
        in_specs=[VMEM] * len(parts),
        out_specs=VMEM,
        out_shape=shape(sum(p.shape[0] for p in parts), *parts[0].shape[1:]),
        compiler_params=PARAMS,
        name="join",
    )(*parts)


def share_kernel(place, keep, other, *outs):
    for k, out in enumerate(outs):
        for i in range(2):
            at = ((place[3] + k) % 4) * 2 + i
            out[i] = (keep[at] + other[at]).astype(out.dtype)


def share(place, keep, other):
    return pl.pallas_call(
        share_kernel,
        in_specs=[SMEM] + [VMEM] * 2,
        out_specs=[VMEM] * 4,
        out_shape=[shape(2, B, B, dtype=F32)] + [shape(2, B, B)] * 3,
        compiler_params=PARAMS,
        name="share",
    )(place, keep, other)


def total_kernel(scale, *refs):
    refs[-1][...] = (sum(r[...].astype(F32) for r in refs[:-1]) * scale).astype(refs[-1].dtype)


def total(parts, scale=1.0):
    return pl.pallas_call(
        functools.partial(total_kernel, scale),
        in_specs=[VMEM] * len(parts),
        out_specs=VMEM,
        out_shape=shape(*parts[0].shape),
        compiler_params=PARAMS,
        name="total",
    )(*parts)


def assemble_kernel(place, *refs):
    mine, twin, out, sems = refs[:4], refs[4:8], refs[8], refs[9]
    y, zl, core, x = place[0], place[1], place[2], place[3]
    copies = []
    for s in range(8):
        within = ((x + 4 - s // 2) % 4) * 2 + s % 2
        for source, half in ((mine, core), (twin, 1 - core)):
            m = half * 8 + within
            to = out.at[((y + 4 - m // 4) % 4) * 4 + (zl + 4 - m % 4) % 4]
            copies.append(pltpu.make_async_copy(source[s // 2].at[s % 2], to, sems.at[len(copies)]))
            copies[-1].start()
    for copy in copies:
        copy.wait()


def assemble(place, mine, twin):
    return pl.pallas_call(
        assemble_kernel,
        in_specs=[SMEM] + [VMEM] * 8,
        out_specs=pl.BlockSpec(memory_space=pltpu.HBM),
        out_shape=shape(16, B, B),
        scratch_shapes=[pltpu.SemaphoreType.DMA((16,))],
        compiler_params=PARAMS,
        name="assemble",
    )(place, *mine, *twin)


def send_on(piece, axis, k):
    return lax.ppermute(piece, axis, ring(k))


def relay_first(parts):
    return send_on(parts[0], "y", 1), send_on(parts[1], "y", 3)


def relay_second(parts, got):
    up, down = relay(*parts[2:6], *got)
    return send_on(up, "y", 1), send_on(down, "y", 3)


def body(hidden, gain, projector, doc_lengths, doc_student, resid, attn, weight):
    groups, slot = 16, attn.shape[0] // 16
    rows = hidden.shape[0]
    me = lax.axis_index(GROUP)
    x, y, zl, core = (lax.axis_index(a) for a in ("x", "y", "zl", "core"))
    place = jnp.stack([y, zl, core, x])

    offsets = jnp.cumsum(doc_lengths, axis=1) - doc_lengths
    matches = (doc_student[me][:, None] == jnp.arange(groups, dtype=jnp.int32)[None, :]).astype(jnp.int32)
    length = jnp.sum(matches * doc_lengths[me][:, None], axis=0)
    offset = jnp.sum(matches * offsets[me][:, None], axis=0)
    position = jnp.arange(slot, dtype=jnp.int32)
    where = jnp.where(position[None, :] < length[:, None], offset[:, None] + position[None, :], -1)

    slots = lax.all_to_all(attn.reshape(groups, slot, B), GROUP, 0, 0, tiled=True)
    teacher = project(place, hidden, gain, projector)
    got = relay_first(teacher)
    attn_rows = pick(where, slots)
    got, _ = tie(got, attn_rows)
    along_zl = [attn_rows] + [send_on(attn_rows, "zl", j) for j in (1, 2, 3)]
    up, down = relay(*teacher[2:6], *got)
    far = send_on(up, "y", 1), send_on(down, "y", 3)
    resid, _ = tie(resid, up)
    resid_slots = lax.all_to_all(resid.reshape(groups, slot, B), GROUP, 0, 0, tiled=True)

    chunk = join(*(p[None] for p in along_zl))
    far, _ = tie(far, chunk)
    chunks = [chunk] + [send_on(chunk, "y", k) for k in (1, 2, 3)]
    folded = fold(teacher[6], *far)
    parts = [folded[0]] + [send_on(folded[j], "zl", j) for j in (1, 2, 3)]

    outs = middle(place, chunks, weight.reshape(16, B, B), where, resid_slots, parts)
    grads, keep, send = outs[:5], outs[5], outs[6]

    got = relay_first(grads)
    other = lax.ppermute(send, "core", SWAP)
    pieces = share(place, keep, other)
    got, _ = tie(got, pieces)
    pieces = [pieces[0]] + [send_on(pieces[k], "x", k) for k in (1, 2, 3)]
    up, down = heavy_relay(grads[2], grads[3], *got)
    far = send_on(up, "y", 1), send_on(down, "y", 3)

    near = total(pieces)
    away = lax.ppermute(near, "zh", SWAP)
    far, near = tie(far, near)
    folded = heavy_fold(grads[4], *got, *far)
    grad_parts = [folded[0]] + [send_on(folded[j], "zl", j) for j in (1, 2, 3)]
    done = total([near, away], 1.0 / (groups * rows))
    grad_parts, _ = tie(grad_parts, done)
    slots = put(where, grad_parts)
    slots = lax.all_to_all(slots.reshape(groups, slot, B), GROUP, 0, 0, tiled=True)
    mine = [done] + [send_on(done, "x", k) for k in (1, 2, 3)]
    twin = [lax.ppermute(p, "core", SWAP) for p in mine]
    weight_grad = assemble(place, mine, twin).reshape(weight.shape)
    return slots.reshape(attn.shape), weight_grad


def solution(mesh):
    fine = Mesh(mesh.devices.reshape(4, 2, 4, 4, 2), ("x", "zh", "y", "zl", "core"))
    return jax.shard_map(
        body,
        mesh=fine,
        in_specs=(
            P(GROUP, TENSOR),
            P(TENSOR),
            P(TENSOR, None),
            P(),
            P(),
            P(GROUP, TENSOR),
            P(GROUP, TENSOR),
            P(None, TENSOR),
        ),
        out_specs=(P(GROUP, TENSOR), P(None, TENSOR)),
        check_vma=False,
    )
```

```python
import functools

import jax
import jax.numpy as jnp
from jax import lax
from jax.experimental import pallas as pl
from jax.experimental.pallas import tpu as pltpu
from jax.sharding import Mesh
from jax.sharding import PartitionSpec as P

DT = 16384
EPS = 1e-05
GROUP = ("x", "zh", "core")
TENSOR = ("y", "zl")
BF = jnp.bfloat16
F32 = jnp.float32
B = 256
VMEM = pl.BlockSpec(memory_space=pltpu.VMEM)
SMEM = pl.BlockSpec(memory_space=pltpu.SMEM)
PARAMS = pltpu.CompilerParams(vmem_limit_bytes=24 * 1024 * 1024)
SWAP = [(0, 1), (1, 0)]


def ring(k):
    return [(i, (i + k) % 4) for i in range(4)]


def tie(*groups):
    return lax.optimization_barrier(groups)


def shape(*dims, dtype=BF):
    return jax.ShapeDtypeStruct(dims, dtype)


def eye_mask(n):
    return lax.broadcasted_iota(jnp.int32, (n, n), 0) == lax.broadcasted_iota(jnp.int32, (n, n), 1)


def power_rows(row, dtype):
    at = lax.broadcasted_iota(jnp.int32, (16, row.shape[1]), 0)
    if dtype == F32:
        return jnp.where(at == 0, row, 0.0)
    high = row.astype(BF).astype(F32)
    rest = row - high
    middle = rest.astype(BF).astype(F32)
    low = rest - middle
    return jnp.where(at == 0, high, jnp.where(at == 1, middle, jnp.where(at == 2, low, 0.0))).astype(BF)


def piece_of(outs, k, j):
    up, down, near_up, near_down, rest_up, rest_down, own = outs
    if k == 0:
        return own, j
    if k == 1:
        return (near_up, j) if j < 2 else (rest_up, j - 2)
    if k == 2:
        return (up, j) if j < 2 else (down, j - 2)
    return (rest_down, j) if j < 2 else (near_down, j - 2)


def heavy_piece_of(outs, k, j):
    up, down, near_up, near_down, own = outs
    if k == 0:
        return own, j
    if k == 1:
        return (near_up, j) if j < 2 else (up, j)
    if k == 2:
        return (up, j) if j < 2 else (down, j - 2)
    return (down, 2 + j) if j < 2 else (near_down, j - 2)


def heavy_shapes(rows):
    return [shape(4, rows, B)] * 2 + [shape(2, rows, B, dtype=F32)] * 2 + [shape(4, rows, B, dtype=F32)]


def piece_shapes(rows, own=F32):
    return [shape(2, rows, B)] * 2 + [shape(2, rows, B, dtype=F32)] * 2 + [shape(2, rows, B)] * 2 + [shape(4, rows, B, dtype=own)]


def project_kernel(place, hidden, gain, projector, *rest):
    outs, scaled, held, blocks, sems = rest[:7], rest[7], rest[8], rest[9], rest[10]
    y, zl = place[0], place[1]
    width = blocks.shape[2]
    first = pltpu.make_async_copy(hidden, held, sems.at[4])
    first.start()
    copies = []
    for k in range(4):
        at = pl.ds(pl.multiple_of(((y + k) % 4) * width, width), width)
        copies.append(pltpu.make_async_copy(projector.at[:, at], blocks.at[k], sems.at[k]))
        copies[k].start()
    scale = gain[...].astype(F32)
    scale = jnp.concatenate([scale[i : i + 1, :] for i in range(scale.shape[0])], axis=1)
    first.wait()
    wide = held[...].astype(F32)
    scaled[...] = (wide * scale).astype(BF)
    power = jnp.sum(wide * wide, axis=1, keepdims=True)
    power = jnp.sum(jnp.where(eye_mask(B), power, 0.0), axis=0, keepdims=True)
    for out in outs:
        rows = power_rows(power, out.dtype)
        for i in range(out.shape[0]):
            out[i, B:, :] = rows
    for k in range(4):
        copies[k].wait()
        for j in range(4):
            out, i = piece_of(outs, k, j)
            at = pl.ds(pl.multiple_of(((zl + j) % 4) * B, B), B)
            out[i, :B, :] = jnp.dot(scaled[...], blocks[k, :, at], preferred_element_type=F32).astype(out.dtype)


def project(place, hidden, gain, projector):
    rows, depth = hidden.shape
    width = projector.shape[1] // 4
    hbm = pl.BlockSpec(memory_space=pltpu.HBM)
    return pl.pallas_call(
        project_kernel,
        in_specs=[SMEM, hbm, VMEM, hbm],
        out_specs=[VMEM] * 7,
        out_shape=piece_shapes(rows + 16, BF),
        scratch_shapes=[
            pltpu.VMEM((rows, depth), BF),
            pltpu.VMEM((rows, depth), BF),
            pltpu.VMEM((4, depth, width), BF),
            pltpu.SemaphoreType.DMA((5,)),
        ],
        compiler_params=pltpu.CompilerParams(vmem_limit_bytes=48 * 1024 * 1024),
        cost_estimate=pl.CostEstimate(
            flops=2 * rows * depth * 4 * width, bytes_accessed=2 * depth * 4 * width, transcendentals=0
        ),
        name="project",
    )(place, hidden, gain.reshape(depth // 128, 128), projector)


def put_sum(out, at, terms):
    rows = terms[0].shape[0]
    total = sum(t[:B, :].astype(F32) for t in terms).astype(out.dtype)
    if at is None:
        out[:B, :] = total
    else:
        out[at, :B, :] = total
    if rows > B:
        power = sum(jnp.sum(t[B:, :].astype(F32), axis=0, keepdims=True) for t in terms)
        power = power_rows(power, out.dtype)
        if at is None:
            out[B:, :] = power
        else:
            out[at, B:, :] = power


def relay_kernel(near_up, near_down, rest_up, rest_down, got_up, got_down, up, down):
    for i in range(2):
        put_sum(up, i, [near_up.at[i], got_up.at[i]])
        put_sum(down, 2 + i, [near_down.at[i], got_down.at[i]])
        up[2 + i] = rest_up[i]
        down[i] = rest_down[i]


def relay(*parts):
    rows = parts[0].shape[1]
    return pl.pallas_call(
        relay_kernel,
        in_specs=[VMEM] * 6,
        out_specs=[VMEM] * 2,
        out_shape=[shape(4, rows, B)] * 2,
        compiler_params=PARAMS,
        name="relay",
    )(*parts)


def heavy_relay_kernel(near_up, near_down, got_up, got_down, up, down):
    for i in range(2):
        put_sum(up, i, [near_up.at[i], got_up.at[i]])
        put_sum(down, i, [near_down.at[i], got_down.at[i]])


def heavy_relay(*parts):
    return pl.pallas_call(
        heavy_relay_kernel,
        in_specs=[VMEM] * 4,
        out_specs=[VMEM] * 2,
        out_shape=[shape(2, B, B)] * 2,
        compiler_params=PARAMS,
        name="heavy_relay",
    )(*parts)


def heavy_fold_kernel(own, got_up, got_down, far_up, far_down, *outs):
    for j, out in enumerate(outs):
        got, far = (got_down.at[2 + j], far_up.at[j]) if j < 2 else (got_up.at[j], far_down.at[j - 2])
        put_sum(out, None, [own.at[j], got, far])


def heavy_fold(*parts):
    return pl.pallas_call(
        heavy_fold_kernel,
        in_specs=[VMEM] * 5,
        out_specs=[VMEM] * 4,
        out_shape=[shape(B, B, dtype=F32)] + [shape(B, B)] * 3,
        compiler_params=PARAMS,
        name="heavy_fold",
    )(*parts)


def fold_kernel(own, far_up, far_down, *outs):
    for j, out in enumerate(outs):
        put_sum(out, None, [own.at[j], far_up.at[j], far_down.at[j]])


def fold(*parts):
    rows = parts[0].shape[1]
    return pl.pallas_call(
        fold_kernel,
        in_specs=[VMEM] * 3,
        out_specs=[VMEM] * 4,
        out_shape=[shape(rows, B, dtype=F32)] + [shape(rows, B)] * 3,
        compiler_params=PARAMS,
        name="fold",
    )(*parts)


def middle_kernel(place, a0, a1, a2, a3, weight, resid, t0, t1, t2, t3, *outs):
    pieces, keep, send = outs[:5], outs[5], outs[6]
    y, zl, core = place[0], place[1], place[2]
    attn = (a0, a1, a2, a3)
    parts = (t0, t1, t2, t3)
    total = sum(r[:B, :].astype(F32) for r in parts)
    power = jnp.sum(sum(r[B:, :].astype(F32) for r in parts), axis=0, keepdims=True)
    power = jnp.sum(jnp.where(eye_mask(B), power, 0.0), axis=1, keepdims=True)
    value = resid[...].astype(F32) - total * lax.rsqrt(power / DT + EPS)
    for k in range(4):
        for j in range(4):
            w = weight[((y + 4 - k) % 4) * 4 + (zl + 4 - j) % 4]
            value += jnp.dot(attn[k][j], w, preferred_element_type=F32)
    residual = value.astype(BF)
    for k in range(4):
        for j in range(4):
            out, i = heavy_piece_of(pieces, k, j)
            w = weight[((y + k) % 4) * 4 + (zl + j) % 4]
            out[i] = lax.dot_general(
                residual, w, (((1,), (1,)), ((), ())), preferred_element_type=F32
            ).astype(out.dtype)
    for half in range(2):

        @pl.when(core == half)
        def _(half=half):
            for m in range(16):
                out = keep if m // 8 == half else send
                out[m % 8] = lax.dot_general(
                    attn[m // 4][m % 4], residual, (((0,), (0,)), ((), ())), preferred_element_type=F32
                ).astype(out.dtype)


def middle(place, chunks, weight, resid, parts):
    return pl.pallas_call(
        middle_kernel,
        in_specs=[SMEM] + [VMEM] * 10,
        out_specs=[VMEM] * 7,
        out_shape=heavy_shapes(B) + [shape(8, B, B, dtype=F32)] * 2,
        compiler_params=PARAMS,
        name="middle",
    )(place, *chunks, weight, resid, *parts)


def pick_kernel(at, slots, out):
    rows = lax.broadcasted_iota(jnp.int32, (B, slots.shape[0]), 0)
    select = jnp.where(rows == at[...], 1.0, 0.0).astype(BF)
    out[...] = jnp.dot(select, slots[...], preferred_element_type=F32).astype(BF)


def pick(at, slots):
    return pl.pallas_call(
        pick_kernel,
        in_specs=[VMEM] * 2,
        out_specs=VMEM,
        out_shape=shape(B, B),
        compiler_params=PARAMS,
        name="pick",
    )(at.reshape(1, -1), slots.reshape(-1, B))


def put_kernel(at, a, b, c, d, out):
    grad = sum(r[...].astype(F32) for r in (a, b, c, d)).astype(BF)
    rows = lax.broadcasted_iota(jnp.int32, (out.shape[0], B), 1)
    select = jnp.where(rows == at[...], 1.0, 0.0).astype(BF)
    out[...] = jnp.dot(select, grad, preferred_element_type=F32).astype(BF)


def put(at, parts):
    at = at.reshape(-1)
    return pl.pallas_call(
        put_kernel,
        in_specs=[VMEM] * 5,
        out_specs=VMEM,
        out_shape=shape(at.shape[0], B),
        compiler_params=PARAMS,
        name="put",
    )(at.reshape(-1, 1), *parts)


def join_kernel(*refs):
    out, i = refs[-1], 0
    for ref in refs[:-1]:
        for j in range(ref.shape[0]):
            out[i] = ref[j]
            i += 1


def join(*parts):
    return pl.pallas_call(
        join_kernel,
        in_specs=[VMEM] * len(parts),
        out_specs=VMEM,
        out_shape=shape(sum(p.shape[0] for p in parts), *parts[0].shape[1:]),
        compiler_params=PARAMS,
        name="join",
    )(*parts)


def share_kernel(place, keep, other, *outs):
    for k, out in enumerate(outs):
        for i in range(2):
            at = ((place[3] + k) % 4) * 2 + i
            out[i] = (keep[at] + other[at]).astype(out.dtype)


def share(place, keep, other):
    return pl.pallas_call(
        share_kernel,
        in_specs=[SMEM] + [VMEM] * 2,
        out_specs=[VMEM] * 4,
        out_shape=[shape(2, B, B, dtype=F32)] + [shape(2, B, B)] * 3,
        compiler_params=PARAMS,
        name="share",
    )(place, keep, other)


def total_kernel(scale, *refs):
    refs[-1][...] = (sum(r[...].astype(F32) for r in refs[:-1]) * scale).astype(refs[-1].dtype)


def total(parts, scale=1.0):
    return pl.pallas_call(
        functools.partial(total_kernel, scale),
        in_specs=[VMEM] * len(parts),
        out_specs=VMEM,
        out_shape=shape(*parts[0].shape),
        compiler_params=PARAMS,
        name="total",
    )(*parts)


def assemble_kernel(place, *refs):
    mine, twin, out, sems = refs[:4], refs[4:8], refs[8], refs[9]
    y, zl, core, x = place[0], place[1], place[2], place[3]
    copies = []
    for s in range(8):
        within = ((x + 4 - s // 2) % 4) * 2 + s % 2
        for source, half in ((mine, core), (twin, 1 - core)):
            m = half * 8 + within
            to = out.at[((y + 4 - m // 4) % 4) * 4 + (zl + 4 - m % 4) % 4]
            copies.append(pltpu.make_async_copy(source[s // 2].at[s % 2], to, sems.at[len(copies)]))
            copies[-1].start()
    for copy in copies:
        copy.wait()


def assemble(place, mine, twin):
    return pl.pallas_call(
        assemble_kernel,
        in_specs=[SMEM] + [VMEM] * 8,
        out_specs=pl.BlockSpec(memory_space=pltpu.HBM),
        out_shape=shape(16, B, B),
        scratch_shapes=[pltpu.SemaphoreType.DMA((16,))],
        compiler_params=PARAMS,
        name="assemble",
    )(place, *mine, *twin)


def send_on(piece, axis, k):
    return lax.ppermute(piece, axis, ring(k))


def relay_first(parts):
    return send_on(parts[0], "y", 1), send_on(parts[1], "y", 3)


def relay_second(parts, got):
    up, down = relay(*parts[2:6], *got)
    return send_on(up, "y", 1), send_on(down, "y", 3)


def body(hidden, gain, projector, doc_lengths, doc_student, resid, attn, weight):
    groups, slot = 16, attn.shape[0] // 16
    rows = hidden.shape[0]
    me = lax.axis_index(GROUP)
    x, y, zl, core = (lax.axis_index(a) for a in ("x", "y", "zl", "core"))
    place = jnp.stack([y, zl, core, x])

    offsets = jnp.cumsum(doc_lengths, axis=1) - doc_lengths
    matches = (doc_student[me][:, None] == jnp.arange(groups, dtype=jnp.int32)[None, :]).astype(jnp.int32)
    length = jnp.sum(matches * doc_lengths[me][:, None], axis=0)
    offset = jnp.sum(matches * offsets[me][:, None], axis=0)
    position = jnp.arange(slot, dtype=jnp.int32)
    where = jnp.where(position[None, :] < length[:, None], offset[:, None] + position[None, :], -1)

    slots = lax.all_to_all(attn.reshape(groups, slot, B), GROUP, 0, 0, tiled=True)
    teacher = project(place, hidden, gain, projector)
    got = relay_first(teacher)
    attn_rows = pick(where, slots)
    got, _ = tie(got, attn_rows)
    along_zl = [attn_rows] + [send_on(attn_rows, "zl", j) for j in (1, 2, 3)]
    up, down = relay(*teacher[2:6], *got)
    far = send_on(up, "y", 1), send_on(down, "y", 3)
    resid, _ = tie(resid, up)
    resid_rows = pick(where, lax.all_to_all(resid.reshape(groups, slot, B), GROUP, 0, 0, tiled=True))

    chunk = join(*(p[None] for p in along_zl))
    far, _ = tie(far, chunk)
    chunks = [chunk] + [send_on(chunk, "y", k) for k in (1, 2, 3)]
    folded = fold(teacher[6], *far)
    parts = [folded[0]] + [send_on(folded[j], "zl", j) for j in (1, 2, 3)]

    outs = middle(place, chunks, weight.reshape(16, B, B), resid_rows, parts)
    grads, keep, send = outs[:5], outs[5], outs[6]

    got = relay_first(grads)
    other = lax.ppermute(send, "core", SWAP)
    pieces = share(place, keep, other)
    got, _ = tie(got, pieces)
    pieces = [pieces[0]] + [send_on(pieces[k], "x", k) for k in (1, 2, 3)]
    up, down = heavy_relay(grads[2], grads[3], *got)
    far = send_on(up, "y", 1), send_on(down, "y", 3)

    near = total(pieces)
    away = lax.ppermute(near, "zh", SWAP)
    far, near = tie(far, near)
    folded = heavy_fold(grads[4], *got, *far)
    grad_parts = [folded[0]] + [send_on(folded[j], "zl", j) for j in (1, 2, 3)]
    done = total([near, away], 1.0 / (groups * rows))
    grad_parts, _ = tie(grad_parts, done)
    slots = put(where, grad_parts)
    slots = lax.all_to_all(slots.reshape(groups, slot, B), GROUP, 0, 0, tiled=True)
    mine = [done] + [send_on(done, "x", k) for k in (1, 2, 3)]
    twin = [lax.ppermute(p, "core", SWAP) for p in mine]
    weight_grad = assemble(place, mine, twin).reshape(weight.shape)
    return slots.reshape(attn.shape), weight_grad


def solution(mesh):
    fine = Mesh(mesh.devices.reshape(4, 2, 4, 4, 2), ("x", "zh", "y", "zl", "core"))
    return jax.shard_map(
        body,
        mesh=fine,
        in_specs=(
            P(GROUP, TENSOR),
            P(TENSOR),
            P(TENSOR, None),
            P(),
            P(),
            P(GROUP, TENSOR),
            P(GROUP, TENSOR),
            P(None, TENSOR),
        ),
        out_specs=(P(GROUP, TENSOR), P(None, TENSOR)),
        check_vma=False,
    )
```

```python
import functools

import jax
import jax.numpy as jnp
from jax import lax
from jax.experimental import pallas as pl
from jax.experimental.pallas import tpu as pltpu
from jax.sharding import Mesh
from jax.sharding import PartitionSpec as P

DT = 16384
EPS = 1e-05
GROUP = ("x", "zh", "core")
TENSOR = ("y", "zl")
BF = jnp.bfloat16
F32 = jnp.float32
B = 256
VMEM = pl.BlockSpec(memory_space=pltpu.VMEM)
SMEM = pl.BlockSpec(memory_space=pltpu.SMEM)
PARAMS = pltpu.CompilerParams(vmem_limit_bytes=24 * 1024 * 1024)
SWAP = [(0, 1), (1, 0)]


def ring(k):
    return [(i, (i + k) % 4) for i in range(4)]


def tie(*groups):
    return lax.optimization_barrier(groups)


def shape(*dims, dtype=BF):
    return jax.ShapeDtypeStruct(dims, dtype)


def eye_mask(n):
    return lax.broadcasted_iota(jnp.int32, (n, n), 0) == lax.broadcasted_iota(jnp.int32, (n, n), 1)


def power_rows(row, dtype):
    at = lax.broadcasted_iota(jnp.int32, (16, row.shape[1]), 0)
    if dtype == F32:
        return jnp.where(at == 0, row, 0.0)
    high = row.astype(BF).astype(F32)
    rest = row - high
    middle = rest.astype(BF).astype(F32)
    low = rest - middle
    return jnp.where(at == 0, high, jnp.where(at == 1, middle, jnp.where(at == 2, low, 0.0))).astype(BF)


def piece_of(outs, k, j):
    up, down, near_up, near_down, rest_up, rest_down, own = outs
    if k == 0:
        return own, j
    if k == 1:
        return (near_up, j) if j < 2 else (rest_up, j - 2)
    if k == 2:
        return (up, j) if j < 2 else (down, j - 2)
    return (rest_down, j) if j < 2 else (near_down, j - 2)


def heavy_piece_of(outs, k, j):
    up, down, near_up, near_down, own = outs
    if k == 0:
        return own, j
    if k == 1:
        return (near_up, j) if j < 2 else (up, j)
    if k == 2:
        return (up, j) if j < 2 else (down, j - 2)
    return (down, 2 + j) if j < 2 else (near_down, j - 2)


def heavy_shapes(rows):
    return [shape(4, rows, B)] * 2 + [shape(2, rows, B, dtype=F32)] * 2 + [shape(4, rows, B, dtype=F32)]


def piece_shapes(rows, own=F32):
    return [shape(2, rows, B)] * 2 + [shape(2, rows, B, dtype=F32)] * 2 + [shape(2, rows, B)] * 2 + [shape(4, rows, B, dtype=own)]


def project_kernel(place, hidden, gain, projector, *rest):
    outs, scaled, held, blocks, sems = rest[:7], rest[7], rest[8], rest[9], rest[10]
    y, zl = place[0], place[1]
    width = blocks.shape[2]
    first = pltpu.make_async_copy(hidden, held, sems.at[4])
    first.start()
    copies = []
    for k in range(4):
        at = pl.ds(pl.multiple_of(((y + k) % 4) * width, width), width)
        copies.append(pltpu.make_async_copy(projector.at[:, at], blocks.at[k], sems.at[k]))
        copies[k].start()
    scale = gain[...].astype(F32)
    scale = jnp.concatenate([scale[i : i + 1, :] for i in range(scale.shape[0])], axis=1)
    first.wait()
    wide = held[...].astype(F32)
    scaled[...] = (wide * scale).astype(BF)
    power = jnp.sum(wide * wide, axis=1, keepdims=True)
    power = jnp.sum(jnp.where(eye_mask(B), power, 0.0), axis=0, keepdims=True)
    for out in outs:
        rows = power_rows(power, out.dtype)
        for i in range(out.shape[0]):
            out[i, B:, :] = rows
    for k in range(4):
        copies[k].wait()
        for j in range(4):
            out, i = piece_of(outs, k, j)
            at = pl.ds(pl.multiple_of(((zl + j) % 4) * B, B), B)
            out[i, :B, :] = jnp.dot(scaled[...], blocks[k, :, at], preferred_element_type=F32).astype(out.dtype)


def project(place, hidden, gain, projector):
    rows, depth = hidden.shape
    width = projector.shape[1] // 4
    hbm = pl.BlockSpec(memory_space=pltpu.HBM)
    return pl.pallas_call(
        project_kernel,
        in_specs=[SMEM, hbm, VMEM, hbm],
        out_specs=[VMEM] * 7,
        out_shape=piece_shapes(rows + 16, BF),
        scratch_shapes=[
            pltpu.VMEM((rows, depth), BF),
            pltpu.VMEM((rows, depth), BF),
            pltpu.VMEM((4, depth, width), BF),
            pltpu.SemaphoreType.DMA((5,)),
        ],
        compiler_params=pltpu.CompilerParams(vmem_limit_bytes=48 * 1024 * 1024),
        cost_estimate=pl.CostEstimate(
            flops=2 * rows * depth * 4 * width, bytes_accessed=2 * depth * 4 * width, transcendentals=0
        ),
        name="project",
    )(place, hidden, gain.reshape(depth // 128, 128), projector)


def put_sum(out, at, terms):
    rows = terms[0].shape[0]
    total = sum(t[:B, :].astype(F32) for t in terms).astype(out.dtype)
    if at is None:
        out[:B, :] = total
    else:
        out[at, :B, :] = total
    if rows > B:
        power = sum(jnp.sum(t[B:, :].astype(F32), axis=0, keepdims=True) for t in terms)
        power = power_rows(power, out.dtype)
        if at is None:
            out[B:, :] = power
        else:
            out[at, B:, :] = power


def relay_kernel(near_up, near_down, rest_up, rest_down, got_up, got_down, up, down):
    for i in range(2):
        put_sum(up, i, [near_up.at[i], got_up.at[i]])
        put_sum(down, 2 + i, [near_down.at[i], got_down.at[i]])
        up[2 + i] = rest_up[i]
        down[i] = rest_down[i]


def relay(*parts):
    rows = parts[0].shape[1]
    return pl.pallas_call(
        relay_kernel,
        in_specs=[VMEM] * 6,
        out_specs=[VMEM] * 2,
        out_shape=[shape(4, rows, B)] * 2,
        compiler_params=PARAMS,
        name="relay",
    )(*parts)


def heavy_relay_kernel(near_up, near_down, got_up, got_down, up, down):
    for i in range(2):
        put_sum(up, i, [near_up.at[i], got_up.at[i]])
        put_sum(down, i, [near_down.at[i], got_down.at[i]])


def heavy_relay(*parts):
    return pl.pallas_call(
        heavy_relay_kernel,
        in_specs=[VMEM] * 4,
        out_specs=[VMEM] * 2,
        out_shape=[shape(2, B, B)] * 2,
        compiler_params=PARAMS,
        name="heavy_relay",
    )(*parts)


def heavy_fold_kernel(own, got_up, got_down, far_up, far_down, *outs):
    for j, out in enumerate(outs):
        got, far = (got_down.at[2 + j], far_up.at[j]) if j < 2 else (got_up.at[j], far_down.at[j - 2])
        put_sum(out, None, [own.at[j], got, far])


def heavy_fold(*parts):
    return pl.pallas_call(
        heavy_fold_kernel,
        in_specs=[VMEM] * 5,
        out_specs=[VMEM] * 4,
        out_shape=[shape(B, B, dtype=F32)] + [shape(B, B)] * 3,
        compiler_params=PARAMS,
        name="heavy_fold",
    )(*parts)


def fold_kernel(own, far_up, far_down, *outs):
    for j, out in enumerate(outs):
        put_sum(out, None, [own.at[j], far_up.at[j], far_down.at[j]])


def fold(*parts):
    rows = parts[0].shape[1]
    return pl.pallas_call(
        fold_kernel,
        in_specs=[VMEM] * 3,
        out_specs=[VMEM] * 4,
        out_shape=[shape(rows, B, dtype=F32)] + [shape(rows, B)] * 3,
        compiler_params=PARAMS,
        name="fold",
    )(*parts)


def middle_kernel(place, a0, a1, a2, a3, weight, resid, t0, t1, t2, t3, *outs):
    pieces, keep, send = outs[:5], outs[5], outs[6]
    y, zl, core = place[0], place[1], place[2]
    attn = (a0, a1, a2, a3)
    parts = (t0, t1, t2, t3)
    total = sum(r[:B, :].astype(F32) for r in parts)
    power = jnp.sum(sum(r[B:, :].astype(F32) for r in parts), axis=0, keepdims=True)
    power = jnp.sum(jnp.where(eye_mask(B), power, 0.0), axis=1, keepdims=True)
    value = resid[...].astype(F32) - total * lax.rsqrt(power / DT + EPS)
    for k in range(4):
        for j in range(4):
            w = weight[((y + 4 - k) % 4) * 4 + (zl + 4 - j) % 4]
            value += jnp.dot(attn[k][j], w, preferred_element_type=F32)
    residual = value.astype(BF)
    for k in range(4):
        for j in range(4):
            out, i = heavy_piece_of(pieces, k, j)
            w = weight[((y + k) % 4) * 4 + (zl + j) % 4]
            out[i] = lax.dot_general(
                residual, w, (((1,), (1,)), ((), ())), preferred_element_type=F32
            ).astype(out.dtype)
    for half in range(2):

        @pl.when(core == half)
        def _(half=half):
            for m in range(16):
                out = keep if m // 8 == half else send
                out[m % 8] = lax.dot_general(
                    attn[m // 4][m % 4], residual, (((0,), (0,)), ((), ())), preferred_element_type=F32
                ).astype(out.dtype)


def middle(place, chunks, weight, resid, parts):
    return pl.pallas_call(
        middle_kernel,
        in_specs=[SMEM] + [VMEM] * 10,
        out_specs=[VMEM] * 7,
        out_shape=heavy_shapes(B) + [shape(8, B, B, dtype=F32), shape(8, B, B)],
        compiler_params=PARAMS,
        name="middle",
    )(place, *chunks, weight, resid, *parts)


def pick_kernel(at, slots, out):
    rows = lax.broadcasted_iota(jnp.int32, (B, slots.shape[0]), 0)
    select = jnp.where(rows == at[...], 1.0, 0.0).astype(BF)
    out[...] = jnp.dot(select, slots[...], preferred_element_type=F32).astype(BF)


def pick(at, slots):
    return pl.pallas_call(
        pick_kernel,
        in_specs=[VMEM] * 2,
        out_specs=VMEM,
        out_shape=shape(B, B),
        compiler_params=PARAMS,
        name="pick",
    )(at.reshape(1, -1), slots.reshape(-1, B))


def put_kernel(at, a, b, c, d, out):
    grad = sum(r[...].astype(F32) for r in (a, b, c, d)).astype(BF)
    rows = lax.broadcasted_iota(jnp.int32, (out.shape[0], B), 1)
    select = jnp.where(rows == at[...], 1.0, 0.0).astype(BF)
    out[...] = jnp.dot(select, grad, preferred_element_type=F32).astype(BF)


def put(at, parts):
    at = at.reshape(-1)
    return pl.pallas_call(
        put_kernel,
        in_specs=[VMEM] * 5,
        out_specs=VMEM,
        out_shape=shape(at.shape[0], B),
        compiler_params=PARAMS,
        name="put",
    )(at.reshape(-1, 1), *parts)


def join_kernel(*refs):
    out, i = refs[-1], 0
    for ref in refs[:-1]:
        for j in range(ref.shape[0]):
            out[i] = ref[j]
            i += 1


def join(*parts):
    return pl.pallas_call(
        join_kernel,
        in_specs=[VMEM] * len(parts),
        out_specs=VMEM,
        out_shape=shape(sum(p.shape[0] for p in parts), *parts[0].shape[1:]),
        compiler_params=PARAMS,
        name="join",
    )(*parts)


def share_kernel(place, keep, other, *outs):
    for k, out in enumerate(outs):
        for i in range(2):
            at = ((place[3] + k) % 4) * 2 + i
            out[i] = (keep[at] + other[at].astype(F32)).astype(out.dtype)


def share(place, keep, other):
    return pl.pallas_call(
        share_kernel,
        in_specs=[SMEM] + [VMEM] * 2,
        out_specs=[VMEM] * 4,
        out_shape=[shape(2, B, B, dtype=F32)] + [shape(2, B, B)] * 3,
        compiler_params=PARAMS,
        name="share",
    )(place, keep, other)


def total_kernel(scale, *refs):
    refs[-1][...] = (sum(r[...].astype(F32) for r in refs[:-1]) * scale).astype(refs[-1].dtype)


def total(parts, scale=1.0):
    return pl.pallas_call(
        functools.partial(total_kernel, scale),
        in_specs=[VMEM] * len(parts),
        out_specs=VMEM,
        out_shape=shape(*parts[0].shape),
        compiler_params=PARAMS,
        name="total",
    )(*parts)


def assemble_kernel(place, *refs):
    mine, twin, out, sems = refs[:4], refs[4:8], refs[8], refs[9]
    y, zl, core, x = place[0], place[1], place[2], place[3]
    copies = []
    for s in range(8):
        within = ((x + 4 - s // 2) % 4) * 2 + s % 2
        for source, half in ((mine, core), (twin, 1 - core)):
            m = half * 8 + within
            to = out.at[((y + 4 - m // 4) % 4) * 4 + (zl + 4 - m % 4) % 4]
            copies.append(pltpu.make_async_copy(source[s // 2].at[s % 2], to, sems.at[len(copies)]))
            copies[-1].start()
    for copy in copies:
        copy.wait()


def assemble(place, mine, twin):
    return pl.pallas_call(
        assemble_kernel,
        in_specs=[SMEM] + [VMEM] * 8,
        out_specs=pl.BlockSpec(memory_space=pltpu.HBM),
        out_shape=shape(16, B, B),
        scratch_shapes=[pltpu.SemaphoreType.DMA((16,))],
        compiler_params=PARAMS,
        name="assemble",
    )(place, *mine, *twin)


def send_on(piece, axis, k):
    return lax.ppermute(piece, axis, ring(k))


def relay_first(parts):
    return send_on(parts[0], "y", 1), send_on(parts[1], "y", 3)


def relay_second(parts, got):
    up, down = relay(*parts[2:6], *got)
    return send_on(up, "y", 1), send_on(down, "y", 3)


def body(hidden, gain, projector, doc_lengths, doc_student, resid, attn, weight):
    groups, slot = 16, attn.shape[0] // 16
    rows = hidden.shape[0]
    me = lax.axis_index(GROUP)
    x, y, zl, core = (lax.axis_index(a) for a in ("x", "y", "zl", "core"))
    place = jnp.stack([y, zl, core, x])

    offsets = jnp.cumsum(doc_lengths, axis=1) - doc_lengths
    matches = (doc_student[me][:, None] == jnp.arange(groups, dtype=jnp.int32)[None, :]).astype(jnp.int32)
    length = jnp.sum(matches * doc_lengths[me][:, None], axis=0)
    offset = jnp.sum(matches * offsets[me][:, None], axis=0)
    position = jnp.arange(slot, dtype=jnp.int32)
    where = jnp.where(position[None, :] < length[:, None], offset[:, None] + position[None, :], -1)

    slots = lax.all_to_all(attn.reshape(groups, slot, B), GROUP, 0, 0, tiled=True)
    teacher = project(place, hidden, gain, projector)
    got = relay_first(teacher)
    attn_rows = pick(where, slots)
    got, _ = tie(got, attn_rows)
    along_zl = [attn_rows] + [send_on(attn_rows, "zl", j) for j in (1, 2, 3)]
    up, down = relay(*teacher[2:6], *got)
    far = send_on(up, "y", 1), send_on(down, "y", 3)
    resid, _ = tie(resid, up)
    resid_rows = pick(where, lax.all_to_all(resid.reshape(groups, slot, B), GROUP, 0, 0, tiled=True))

    chunk = join(*(p[None] for p in along_zl))
    far, _ = tie(far, chunk)
    chunks = [chunk] + [send_on(chunk, "y", k) for k in (1, 2, 3)]
    folded = fold(teacher[6], *far)
    parts = [folded[0]] + [send_on(folded[j], "zl", j) for j in (1, 2, 3)]

    outs = middle(place, chunks, weight.reshape(16, B, B), resid_rows, parts)
    grads, keep, send = outs[:5], outs[5], outs[6]

    got = relay_first(grads)
    other = lax.ppermute(send, "core", SWAP)
    pieces = share(place, keep, other)
    pieces = [pieces[0]] + [send_on(pieces[k], "x", k) for k in (1, 2, 3)]
    up, down = heavy_relay(grads[2], grads[3], *got)
    far = send_on(up, "y", 1), send_on(down, "y", 3)

    near = total(pieces)
    away = lax.ppermute(near, "zh", SWAP)
    far, near = tie(far, near)
    folded = heavy_fold(grads[4], *got, *far)
    grad_parts = [folded[0]] + [send_on(folded[j], "zl", j) for j in (1, 2, 3)]
    done = total([near, away], 1.0 / (groups * rows))
    grad_parts, _ = tie(grad_parts, done)
    slots = put(where, grad_parts)
    slots = lax.all_to_all(slots.reshape(groups, slot, B), GROUP, 0, 0, tiled=True)
    mine = [done] + [send_on(done, "x", k) for k in (1, 2, 3)]
    twin = [lax.ppermute(p, "core", SWAP) for p in mine]
    weight_grad = assemble(place, mine, twin).reshape(weight.shape)
    return slots.reshape(attn.shape), weight_grad


def solution(mesh):
    fine = Mesh(mesh.devices.reshape(4, 2, 4, 4, 2), ("x", "zh", "y", "zl", "core"))
    return jax.shard_map(
        body,
        mesh=fine,
        in_specs=(
            P(GROUP, TENSOR),
            P(TENSOR),
            P(TENSOR, None),
            P(),
            P(),
            P(GROUP, TENSOR),
            P(GROUP, TENSOR),
            P(None, TENSOR),
        ),
        out_specs=(P(GROUP, TENSOR), P(None, TENSOR)),
        check_vma=False,
    )
```
